256 devices in a mesh: dp: 256 (over x, z, y, core).
Axes of the slice: x: 4, y: 4, z: 8, core: 2. Of those that a mesh axis runs over, the one named last changes fastest.
Arguments:
- image_emb: bfloat16 [131072, 1152], P('dp'), may hold values from -0.75 to 0.75
- text_emb: bfloat16 [131072, 1152], P('dp'), may hold values from -0.75 to 0.75
- log_scale: float32 [1], replicated, may hold values from 1 to 2.3
- logit_bias: float32 [1], replicated, may hold values from -4 to -1
Outputs:
- image_grad: float32 [131072, 1152], P('dp')
- text_grad: float32 [2, 512, 1152], P(None, 'dp')
- row_loss: float32 [131072], P('dp')
The draws below stay inside these ranges and needn't reach their ends.
All inputs are finite; a program needn't handle non-finite values.
Results may differ from the reference program's by a relative error of at most 0.0019.
Values may be sent and summed in bfloat16 or wider, within the bound.
No kernel may reach another device: no remote copies, remote signals or barrier semaphores. Data moves between devices by JAX's collectives and lax.ppermute only.
A program may use at most 64 MiB of HBM per device.

```python
import jax
import jax.numpy as jnp
from jax import lax

D = 1152
ROWS = 512
STEPS = 2
BATCH = 131072
N_DP = 256


def steps_of(key, shape, pieces, least, top_value):
    def one(position, blocks):
        steps = jax.random.uniform(jax.random.fold_in(jax.random.fold_in(key, 6), position), (blocks,), jnp.float32, least / len(pieces), top_value / len(pieces))
        return jnp.repeat(jnp.exp(steps), shape[position] // blocks).reshape((-1,) + (1,) * (len(shape) - position - 1))

    loudness = one(*pieces[0])
    for cut in pieces[1:]:
        loudness = loudness * one(*cut)
    return loudness


def gaussian(rng, dims, scale, reach, cuts=(), held_as=jnp.bfloat16):
    array = scale * jax.random.normal(rng, dims, jnp.float32)
    if cuts:
        array = array * steps_of(rng, dims, cuts, -0.22, 0.18)
    return jnp.clip(array, -reach, reach).astype(held_as)


def setup_inputs(seed: int = 0) -> dict:
    streams_of = jax.random.split(jax.random.key(seed), 5)
    return {
        "image_emb": gaussian(streams_of[0], (BATCH, D), 0.125, 0.75, ((0, 256),)),
        "text_emb": gaussian(streams_of[1], (BATCH, D), 0.125, 0.75, ((0, 256),)),
        "log_scale": jnp.clip(jax.random.uniform(streams_of[2], (1,), jnp.float32, 1.0, 2.3), 1.0, 2.3),
        "logit_bias": jnp.clip(jax.random.uniform(streams_of[3], (1,), jnp.float32, -4.0, -1.0), -4.0, -1.0),
    }


def reference(image_emb, text_emb, log_scale, logit_bias):
    scale = jnp.exp(log_scale[0])
    bias = logit_bias[0]
    images = image_emb.reshape(N_DP, ROWS, D)
    eye = jnp.eye(ROWS, dtype=jnp.float32)
    indices = jnp.arange(N_DP, dtype=jnp.int32)
    image_grad = jnp.zeros((N_DP, ROWS, D), jnp.float32)
    row_loss = jnp.zeros((N_DP, ROWS), jnp.float32)
    texts = []
    for step in range(STEPS):
        owner = step * (N_DP // STEPS)
        block = text_emb[owner * ROWS:(owner + 1) * ROWS]

        def one(carry, item):
            rows, index = item
            logits = scale * jnp.dot(rows, block.T, preferred_element_type=jnp.float32) + bias
            positive = eye * (index == owner).astype(jnp.float32)
            sign = 2.0 * positive - 1.0
            losses = jnp.sum(jax.nn.softplus(-sign * logits), axis=1)
            weights = (jax.nn.sigmoid(logits) - positive).astype(jnp.bfloat16)
            image_term = scale * jnp.dot(weights, block, preferred_element_type=jnp.float32)
            text_term = scale * jnp.dot(weights.T, rows, preferred_element_type=jnp.float32)
            return carry + text_term, (image_term, losses)

        text_total, (image_terms, losses) = lax.scan(one, jnp.zeros((ROWS, D), jnp.float32), (images, indices))
        image_grad = image_grad + image_terms
        row_loss = row_loss + losses
        texts.append(text_total)
    return image_grad.reshape(N_DP * ROWS, D), jnp.stack(texts), row_loss.reshape(N_DP * ROWS)
```

```python
import jax
import jax.numpy as jnp
from jax import lax
from jax.sharding import Mesh, PartitionSpec as P

STEPS = 2
NX, NZ, NY, NC = 4, 8, 4, 2
AXES = ("x", "z", "y", "c")
PLANE = NX * NZ


def device(x, z, y, c):
    return ((x * NZ + z) * NY + y) * NC + c


def local(image, text, log_scale, logit_bias):
    f32, bf16 = jnp.float32, jnp.bfloat16
    scale = jnp.exp(log_scale[0])
    bias = logit_bias[0]
    rows, width = image.shape
    ix, iz, iy, ic = (lax.axis_index(a) for a in AXES)
    per = rows // (PLANE * NY * NC)
    line = PLANE * per

    images = lax.all_gather(image, ("y", "c"), tiled=True)

    k = jnp.arange(rows)
    c_, y_, p_, r_ = k // (rows // NC), k // line % NY, k // per % PLANE, k % per
    source = ((p_ * NY + y_) * NC + c_) * per + r_
    pick = (source[:, None] == k[None, :]).astype(bf16)
    ordered = jnp.dot(pick, text, preferred_element_type=f32).astype(bf16)
    ordered = ordered.reshape(NC, NY, line, width)

    half = jnp.where(ic == 0, ordered[0], lax.ppermute(ordered[1], "c", [(0, 1)]))
    parts = half[0]
    got = []
    for y in (2, 1, 3):
        pairs = [
            (device(x, 0, 0, c), device(x, 0, y, c))
            for x in range(0, NX, NX // STEPS)
            for c in range(NC)
        ]
        got.append(lax.ppermute(half[y], AXES, pairs))
    parts = jnp.where(iy == 0, parts, got[0] + got[1] + got[2])
    spread = lax.all_to_all(parts, ("x", "z"), 0, 0, tiled=True)
    spread = spread.reshape(PLANE, per, width)
    mine = jnp.stack([spread[s * (PLANE // STEPS)] for s in range(STEPS)])
    everywhere = jnp.broadcast_to(mine[None], (PLANE, STEPS, per, width))
    texts = lax.all_to_all(
        everywhere.reshape(PLANE * STEPS * per, width), ("x", "z"), 0, 0, tiled=True
    )
    count = texts.shape[0]

    t = jnp.arange(count)
    step = t // per % STEPS
    column = ((t // (STEPS * per) * NY + iy) * NC + ic) * per + t % per
    owner = (ix == step * (NX // STEPS)) & (iz == 0)
    b = jnp.arange(images.shape[0])
    positive = ((b[:, None] == column[None, :]) & owner[None, :]).astype(f32)
    logits = scale * jnp.dot(images, texts.T, preferred_element_type=f32) + bias
    weights = (jax.nn.sigmoid(logits) - positive).astype(bf16)
    term = lax.dot_general(
        weights, images, (((0,), (0,)), ((), ())), preferred_element_type=f32
    ).astype(bf16)
    terms = lax.all_to_all(term, ("x", "z"), 0, 0, tiled=True)
    terms = terms.reshape(PLANE, STEPS * per, width).astype(f32)
    text_grad = scale * jnp.sum(terms, axis=0).reshape(STEPS, per, width)

    slots = [texts]
    for n in range(1, NY):
        slots.append(lax.ppermute(texts, "y", [(i, (i + n) % NY) for i in range(NY)]))
    core = jnp.concatenate(slots)
    block = jnp.concatenate([core, lax.ppermute(core, "c", [(0, 1), (1, 0)])])
    t = jnp.arange(block.shape[0])
    c_ = (t // (NY * count) + ic) % NC
    y_ = (iy - t // count % NY) % NY
    step = t // per % STEPS
    column = ((t // (STEPS * per) % PLANE * NY + y_) * NC + c_) * per + t % per
    owner = (ix == step * (NX // STEPS)) & (iz == 0) & (iy == 0) & (ic == 0)
    b = jnp.arange(rows)
    positive = ((b[:, None] == column[None, :]) & owner[None, :]).astype(f32)
    logits = scale * jnp.dot(image, block.T, preferred_element_type=f32) + bias
    sign = 2.0 * positive - 1.0
    row_loss = jnp.sum(jax.nn.softplus(-sign * logits), axis=1)
    weights = (jax.nn.sigmoid(logits) - positive).astype(bf16)
    image_grad = scale * jnp.dot(weights, block, preferred_element_type=f32)
    return image_grad, text_grad, row_loss


def solution(mesh):
    mesh = Mesh(mesh.devices.reshape(NX, NZ, NY, NC), AXES)
    in_specs = (P(AXES, None), P(AXES, None), P(), P())
    out_specs = (P(AXES, None), P(None, AXES, None), P(AXES))
    return jax.shard_map(local, mesh=mesh, in_specs=in_specs, out_specs=out_specs, check_vma=False)
```

```python
import functools

import jax
import jax.numpy as jnp
from jax import lax
from jax.experimental import pallas as pl
from jax.experimental.pallas import tpu as pltpu
from jax.sharding import Mesh, PartitionSpec as P

STEPS = 2
NX, NZ, NY, NC = 4, 8, 4, 2
AXES = ("x", "z", "y", "c")
PLANE = NX * NZ
f32, bf16, i32 = jnp.float32, jnp.bfloat16, jnp.int32
VMEM = pl.BlockSpec(memory_space=pltpu.VMEM)
SMEM = pl.BlockSpec(memory_space=pltpu.SMEM)


def device(x, z, y, c):
    return ((x * NZ + z) * NY + y) * NC + c


def around(a, way):
    pairs = [
        (y * NC + c, (y + way * (1 - 2 * c)) % NY * NC + c) for y in range(NY) for c in range(NC)
    ]
    return lax.ppermute(a, ("y", "c"), pairs)


def along_y(a, shift):
    return lax.ppermute(a, "y", [(i, (i + shift) % NY) for i in range(NY)])


def other_core(a):
    return lax.ppermute(a, "c", [(0, 1), (1, 0)])


def call(body, outs, args, flops=0, scalars=1, **options):
    moved = sum(a.size * a.dtype.itemsize for a in (*args, *outs))
    single = len(outs) == 1
    return pl.pallas_call(
        body,
        out_shape=outs[0] if single else outs,
        in_specs=options.pop("in_specs", [SMEM] * scalars + [VMEM] * (len(args) - scalars)),
        out_specs=VMEM if single else [VMEM] * len(outs),
        compiler_params=pltpu.CompilerParams(vmem_limit_bytes=48 * 2**20),
        cost_estimate=pl.CostEstimate(flops=flops, bytes_accessed=moved, transcendentals=0),
        **options,
    )(*args)


def shaped(*shape, dtype=bf16):
    return jax.ShapeDtypeStruct(shape, dtype)


def slices_kernel(place, text, *refs):
    *outs, sems = refs
    span = outs[0].shape[0]
    copies = []
    for n, out in enumerate(outs):
        at = pl.multiple_of((place[0] + n) % NX * span, span)
        copies.append(pltpu.make_async_copy(text.at[pl.ds(at, span), :], out, sems.at[n]))
        copies[-1].start()
    for copy in copies:
        copy.wait()


def join_kernel(place, *refs):
    *got, out = refs
    x, c = place[0], place[3]
    per = out.shape[1] // STEPS

    def fill(at, core):
        for s in range(STEPS):
            source = got[core * NX + (at - s * (NX // STEPS)) % NX]
            for p in range(out.shape[0]):
                first = (p * NC + core) * per
                out[p, s * per:(s + 1) * per, :] = source[first:first + per, :]

    for at in range(NX):
        for core in range(NC):
            pl.when((x == at) & (c == core))(functools.partial(fill, at, core))


def flat_kernel(chunks, out):
    n = chunks.shape[1]
    for p in range(chunks.shape[0]):
        out[p * n:(p + 1) * n, :] = chunks[p]


def text_row(t, y, c, per):
    return t // per % STEPS, ((t // (STEPS * per) * NY + y) * NC + c) * per + t % per


def term_kernel(turns, place, factors, own, other, *refs):
    images, rest = refs[:len(turns)], refs[len(turns):]
    x, z, y, c = (place[n] for n in range(4))
    scale, bias = factors[0], factors[1]
    count = own.shape[0]
    per = count // (PLANE * STEPS)
    block = jnp.concatenate([own[...], other[...]], axis=0)
    last = len(rest) > 1
    total = rest[0][...] if last else None
    for image, turn in zip(images, turns, strict=True):
        rows = image.shape[0]
        logits = scale * lax.dot_general(
            block, image[...], (((1,), (1,)), ((), ())), preferred_element_type=f32
        ) + bias
        t = lax.broadcasted_iota(i32, (NC * count, 1), 0)
        step, row = text_row(t % count, y, (c + t // count) % NC, per)
        held = (z == 0) & (c == 0) & ((y + turn) % NY == 0)
        row = jnp.where(held & (step * (NX // STEPS) == x), row, -1)
        b = lax.broadcasted_iota(i32, (NC * count, rows), 1)
        weights = (jax.nn.sigmoid(logits) - (b == row).astype(f32)).astype(bf16)
        term = jnp.dot(weights, image[...], preferred_element_type=f32)
        total = term if total is None else total + term
    if last:
        rest[1][...] = total[:count]
        rest[2][...] = total[count:].astype(bf16)
    else:
        rest[0][...] = total


def add_kernel(mine, received, out):
    n = out.shape[1]
    total = (mine[...] + received[...].astype(f32)).astype(bf16)
    for p in range(out.shape[0]):
        out[p] = total[p * n:(p + 1) * n, :]


def sum_kernel(factors, terms, out):
    total = terms[0].astype(f32)
    for p in range(1, terms.shape[0]):
        total = total + terms[p].astype(f32)
    total = factors[0] * total
    per = out.shape[1]
    for s in range(STEPS):
        out[s] = total[s * per:(s + 1) * per, :]


def image_kernel(place, factors, image, *refs):
    *texts, grad, loss = refs
    x, z, y, c = (place[n] for n in range(4))
    scale, bias = factors[0], factors[1]
    rows = image.shape[0]
    count = texts[0].shape[0]
    per = count // (PLANE * STEPS)
    held = (z == 0) & (y == 0) & (c == 0)
    total = losses = None
    for n in range(NY):
        block = jnp.concatenate([texts[n][...], texts[NY + n][...]], axis=0)
        logits = scale * lax.dot_general(
            image[...], block, (((1,), (1,)), ((), ())), preferred_element_type=f32
        ) + bias
        t = lax.broadcasted_iota(i32, (1, NC * count), 1)
        step, row = text_row(t % count, (y + NY - n) % NY, (c + t // count) % NC, per)
        row = jnp.where(held & (step * (NX // STEPS) == x), row, -1)
        b = lax.broadcasted_iota(i32, (rows, NC * count), 0)
        positive = b == row
        e = jnp.exp(-jnp.abs(logits))
        signed = jnp.where(positive, -logits, logits)
        part = jnp.sum(jnp.maximum(signed, 0.0) + jnp.log1p(e), axis=1)
        sigmoid = jnp.where(logits >= 0, 1.0, e) / (1.0 + e)
        weights = (sigmoid - positive.astype(f32)).astype(bf16)
        term = jnp.dot(weights, block, preferred_element_type=f32)
        total = term if total is None else total + term
        losses = part if losses is None else losses + part
    grad[...] = scale * total
    loss[...] = losses


def local(image, text, log_scale, logit_bias):
    rows, width = image.shape
    place = jnp.stack([lax.axis_index(a) for a in AXES]).astype(i32)
    factors = jnp.concatenate([jnp.exp(log_scale), logit_bias])
    per = rows // (PLANE * NY * NC)
    count = PLANE * STEPS * per
    side = NZ * NY * per

    pieces = call(
        slices_kernel,
        [shaped(side * NC, width)] * NX,
        (place, text),
        in_specs=[SMEM, pl.BlockSpec(memory_space=pl.ANY)],
        scratch_shapes=[pltpu.SemaphoreType.DMA((NX,))],
    )
    got = [pieces[0]] + [None] * (NX - 1)
    for n in (2, 1, 3):
        pairs = [
            (device(x, 0, 0, 0), device((x + n) % NX, 0, 0, 0)) for x in range(0, NX, NX // STEPS)
        ]
        got[n] = lax.ppermute(pieces[n], AXES, pairs)
    got += [lax.ppermute(a, "c", [(0, 1)]) for a in got]
    joined = call(join_kernel, [shaped(NZ * NY, STEPS * per, width)], (place, *got))

    images = [image, around(image, 1), around(image, -1)]
    images.append(around(images[1], 1))

    spread = lax.all_to_all(joined, ("z", "y"), 0, 0, tiled=True)
    everywhere = jnp.broadcast_to(spread[:1], (PLANE, STEPS * per, width))
    everywhere, images[1] = lax.optimization_barrier((everywhere, images[1]))
    chunks = lax.all_to_all(everywhere, ("x", "z"), 0, 0, tiled=True)
    texts = call(flat_kernel, [shaped(count, width)], (chunks,), scalars=0)

    other = other_core(texts)
    turns = (0, NY - 1, 1, 2)
    flops = 4 * rows * NC * count * width
    early = call(
        functools.partial(term_kernel, turns[:3]),
        [shaped(NC * count, width, dtype=f32)],
        (place, factors, texts, other, *images[:3]),
        flops=3 * flops,
        scalars=2,
    )
    mine, theirs = call(
        functools.partial(term_kernel, turns[3:]),
        [shaped(count, width, dtype=f32), shaped(count, width)],
        (place, factors, texts, other, *images[3:], early),
        flops=flops,
        scalars=2,
    )
    term = call(
        add_kernel, [shaped(PLANE, STEPS * per, width)], (mine, other_core(theirs)), scalars=0
    )
    terms = lax.all_to_all(term, ("x", "z"), 0, 0, tiled=True)
    text_grad = call(sum_kernel, [shaped(STEPS, per, width, dtype=f32)], (factors, terms))

    line = [texts] + [along_y(texts, n) for n in range(1, NY)]
    across = [other] + [other_core(a) for a in line[1:]]
    image_grad, row_loss = call(
        image_kernel,
        [shaped(rows, width, dtype=f32), shaped(rows, dtype=f32)],
        (place, factors, image, *line, *across),
        flops=NY * flops,
        scalars=2,
    )
    return image_grad, text_grad, row_loss


def solution(mesh):
    mesh = Mesh(mesh.devices.reshape(NX, NZ, NY, NC), AXES)
    in_specs = (P(AXES, None), P(AXES, None), P(), P())
    out_specs = (P(AXES, None), P(None, AXES, None), P(AXES))
    return jax.shard_map(local, mesh=mesh, in_specs=in_specs, out_specs=out_specs, check_vma=False)
```

```python
import functools

import jax
import jax.numpy as jnp
from jax import lax
from jax.experimental import pallas as pl
from jax.experimental.pallas import tpu as pltpu
from jax.sharding import Mesh, PartitionSpec as P

STEPS = 2
NX, NZ, NY, NC = 4, 8, 4, 2
AXES = ("x", "z", "y", "c")
PLANE = NX * NZ
f32, bf16, i32 = jnp.float32, jnp.bfloat16, jnp.int32
VMEM = pl.BlockSpec(memory_space=pltpu.VMEM)
SMEM = pl.BlockSpec(memory_space=pltpu.SMEM)


def device(x, z, y, c):
    return ((x * NZ + z) * NY + y) * NC + c


def around(a, way):
    pairs = [
        (y * NC + c, (y + way * (1 - 2 * c)) % NY * NC + c) for y in range(NY) for c in range(NC)
    ]
    return lax.ppermute(a, ("y", "c"), pairs)


def along_y(a, shift):
    return lax.ppermute(a, "y", [(i, (i + shift) % NY) for i in range(NY)])


def other_core(a):
    return lax.ppermute(a, "c", [(0, 1), (1, 0)])


def call(body, outs, args, flops=0, scalars=1, **options):
    moved = sum(a.size * a.dtype.itemsize for a in (*args, *outs))
    single = len(outs) == 1
    return pl.pallas_call(
        body,
        out_shape=outs[0] if single else outs,
        in_specs=options.pop("in_specs", [SMEM] * scalars + [VMEM] * (len(args) - scalars)),
        out_specs=VMEM if single else [VMEM] * len(outs),
        compiler_params=pltpu.CompilerParams(vmem_limit_bytes=16 * 2**20),
        cost_estimate=pl.CostEstimate(flops=flops, bytes_accessed=moved, transcendentals=0),
        **options,
    )(*args)


def shaped(*shape, dtype=bf16):
    return jax.ShapeDtypeStruct(shape, dtype)


def take_rows(source, c, outs):
    n = outs[0].shape[1]
    count = outs[0].shape[0] * n
    span = NC * count
    per = n * len(outs) // NX
    i = lax.broadcasted_iota(i32, (count, span), 0)
    j = lax.broadcasted_iota(i32, (count, span), 1)
    wanted = (i // per % (n // per)) * (span * len(outs) // NX) + (i // n * NC + c) * per + i % per
    pick = (j == wanted).astype(bf16)
    for h, out in enumerate(outs):
        half = jnp.dot(
            pick, source[h * span:(h + 1) * span, :], preferred_element_type=f32
        ).astype(bf16)
        for p in range(out.shape[0]):
            out[p] = half[p * n:(p + 1) * n, :]


def own_rows_kernel(text, *outs):
    take_rows(text, 0, outs)


def core_rows_kernel(place, received, keep, send, *outs):
    @pl.when(place[3] == 0)
    def _():
        outs[0][...] = keep[...]
        outs[1][...] = send[...]

    @pl.when(place[3] != 0)
    def _():
        take_rows(received, 1, outs)


def flat_kernel(place, chunks, out):
    n = chunks.shape[1]
    per = n // 2

    def fill(core):
        for x in range(NX):
            for z in range(NZ):
                for s in range(STEPS):
                    held = s * (NX // STEPS)
                    if x >= NX // 2:
                        held = (held + (-1 if core else 1)) % NX
                    first = x % (NX // 2) * per
                    at = ((x * NZ + z) * STEPS + s) * per
                    out[at:at + per, :] = chunks[held * NZ + z, first:first + per, :]

    for core in range(NC):
        pl.when(place[3] == core)(functools.partial(fill, core))


def choose_kernel(place, keep, moved, out):
    owner = place[0] % (NX // STEPS) == 0

    @pl.when(owner)
    def _():
        out[...] = keep[...]

    @pl.when(jnp.logical_not(owner))
    def _():
        out[...] = moved[...]


def text_row(t, y, c, per):
    return t // per % STEPS, ((t // (STEPS * per) * NY + y) * NC + c) * per + t % per


def term_kernel(turns, place, factors, own, other, *refs):
    images, rest = refs[:len(turns)], refs[len(turns):]
    x, z, y, c = (place[n] for n in range(4))
    scale, bias = factors[0], factors[1]
    count = own.shape[0]
    per = count // (PLANE * STEPS)
    block = jnp.concatenate([own[...], other[...]], axis=0)
    last = len(rest) > 1
    total = rest[0][...] if last else None
    for image, turn in zip(images, turns, strict=True):
        rows = image.shape[0]
        logits = scale * lax.dot_general(
            block, image[...], (((1,), (1,)), ((), ())), preferred_element_type=f32
        ) + bias
        t = lax.broadcasted_iota(i32, (NC * count, 1), 0)
        step, row = text_row(t % count, y, (c + t // count) % NC, per)
        held = (z == 0) & (c == 0) & ((y + turn) % NY == 0)
        row = jnp.where(held & (step * (NX // STEPS) == x), row, -1)
        b = lax.broadcasted_iota(i32, (NC * count, rows), 1)
        weights = (jax.nn.sigmoid(logits) - (b == row).astype(f32)).astype(bf16)
        term = jnp.dot(weights, image[...], preferred_element_type=f32)
        total = term if total is None else total + term
    if last:
        rest[1][...] = total[:count]
        rest[2][...] = total[count:].astype(bf16)
    else:
        rest[0][...] = total


def add_kernel(mine, received, out):
    n = out.shape[1]
    total = (mine[...] + received[...].astype(f32)).astype(bf16)
    for p in range(out.shape[0]):
        out[p] = total[p * n:(p + 1) * n, :]


def sum_kernel(factors, terms, out):
    total = terms[0].astype(f32)
    for p in range(1, terms.shape[0]):
        total = total + terms[p].astype(f32)
    total = factors[0] * total
    per = out.shape[1]
    for s in range(STEPS):
        out[s] = total[s * per:(s + 1) * per, :]


def image_kernel(place, factors, image, *refs):
    *texts, grad, loss = refs
    x, z, y, c = (place[n] for n in range(4))
    scale, bias = factors[0], factors[1]
    rows = image.shape[0]
    count = texts[0].shape[0]
    per = count // (PLANE * STEPS)
    held = (z == 0) & (y == 0) & (c == 0)
    losses = None
    kept = []
    blocks = [jnp.concatenate([texts[n][...], texts[NY + n][...]], axis=0) for n in range(NY)]
    for n, block in enumerate(blocks):
        logits = scale * lax.dot_general(
            image[...], block, (((1,), (1,)), ((), ())), preferred_element_type=f32
        ) + bias
        t = lax.broadcasted_iota(i32, (1, NC * count), 1)
        step, row = text_row(t % count, (y + NY - n) % NY, (c + t // count) % NC, per)
        row = jnp.where(held & (step * (NX // STEPS) == x), row, -1)
        b = lax.broadcasted_iota(i32, (rows, NC * count), 0)
        positive = b == row
        e = jnp.exp(-jnp.abs(logits))
        signed = jnp.where(positive, -logits, logits)
        part = jnp.maximum(signed, 0.0) + jnp.log1p(e)
        sigmoid = jnp.where(logits >= 0, 1.0, e) / (1.0 + e)
        kept.append((sigmoid - positive.astype(f32)).astype(bf16))
        losses = part if losses is None else losses + part
    weights = jnp.concatenate(kept, axis=1)
    total = jnp.dot(weights, jnp.concatenate(blocks, axis=0), preferred_element_type=f32)
    grad[...] = scale * total
    loss[...] = jnp.sum(losses, axis=1)


def local(image, text, log_scale, logit_bias):
    rows, width = image.shape
    place = jnp.stack([lax.axis_index(a) for a in AXES]).astype(i32)
    factors = jnp.concatenate([jnp.exp(log_scale), logit_bias])
    per = rows // (PLANE * NY * NC)
    count = PLANE * STEPS * per

    chunk = shaped(NZ * NY, STEPS * per, width)
    received = lax.ppermute(text, "c", [(0, 1)])
    own = call(own_rows_kernel, [chunk] * 2, (text,), scalars=0)
    keep, send = call(core_rows_kernel, [chunk] * 2, (place, received, *own))
    owners = range(0, NX, NX // STEPS)
    pairs = [
        (device(x, 0, 0, c), device((x + 1 - 2 * c) % NX, 0, 0, c)) for x in owners for c in range(NC)
    ]
    moved = lax.ppermute(send, AXES, pairs)
    joined = call(choose_kernel, [chunk], (place, keep, moved))

    images = [image, around(image, 1)]
    again, images[1] = lax.optimization_barrier((image, images[1]))
    images += [around(again, -1), around(images[1], 1)]

    spread = lax.all_to_all(joined, ("z", "y"), 0, 0, tiled=True)
    everywhere = jnp.broadcast_to(spread[:1], (PLANE, STEPS * per, width))
    everywhere, images[1] = lax.optimization_barrier((everywhere, images[1]))
    chunks = lax.all_to_all(everywhere, ("x", "z"), 0, 0, tiled=True)
    texts = call(
        flat_kernel,
        [shaped(count, width)],
        (place, chunks),
    )

    other = other_core(texts)
    turns = (0, NY - 1, 1, 2)
    flops = 4 * rows * NC * count * width
    early = call(
        functools.partial(term_kernel, turns[:2]),
        [shaped(NC * count, width, dtype=f32)],
        (place, factors, texts, other, *images[:2]),
        flops=2 * flops,
        scalars=2,
    )
    mine, theirs = call(
        functools.partial(term_kernel, turns[2:]),
        [shaped(count, width, dtype=f32), shaped(count, width)],
        (place, factors, texts, other, *images[2:], early),
        flops=2 * flops,
        scalars=2,
    )
    line = [texts] + [along_y(texts, n) for n in range(1, NY)]
    passed = other_core(theirs)
    passed, line[1], line[3] = lax.optimization_barrier((passed, line[1], line[3]))
    term = call(add_kernel, [shaped(PLANE, STEPS * per, width)], (mine, passed), scalars=0)
    terms = lax.all_to_all(term, ("x", "z"), 0, 0, tiled=True)
    text_grad = call(sum_kernel, [shaped(STEPS, per, width, dtype=f32)], (factors, terms))

    across = [other] + [other_core(a) for a in line[1:]]
    image_grad, row_loss = call(
        image_kernel,
        [shaped(rows, width, dtype=f32), shaped(rows, dtype=f32)],
        (place, factors, image, *line, *across),
        flops=NY * flops,
        scalars=2,
    )
    return image_grad, text_grad, row_loss


def solution(mesh):
    mesh = Mesh(mesh.devices.reshape(NX, NZ, NY, NC), AXES)
    in_specs = (P(AXES, None), P(AXES, None), P(), P())
    out_specs = (P(AXES, None), P(None, AXES, None), P(AXES))
    return jax.shard_map(local, mesh=mesh, in_specs=in_specs, out_specs=out_specs, check_vma=False)
```

```python
import functools

import jax
import jax.numpy as jnp
from jax import lax
from jax.experimental import pallas as pl
from jax.experimental.pallas import tpu as pltpu
from jax.sharding import Mesh, PartitionSpec as P

STEPS = 2
NX, NZ, NY, NC = 4, 8, 4, 2
AXES = ("x", "z", "y", "c")
PLANE = NX * NZ
f32, bf16, i32 = jnp.float32, jnp.bfloat16, jnp.int32
VMEM = pl.BlockSpec(memory_space=pltpu.VMEM)
SMEM = pl.BlockSpec(memory_space=pltpu.SMEM)


def device(x, z, y, c):
    return ((x * NZ + z) * NY + y) * NC + c


def around(a, way):
    pairs = [
        (y * NC + c, (y + way * (2 * c - 1)) % NY * NC + c) for y in range(NY) for c in range(NC)
    ]
    return lax.ppermute(a, ("y", "c"), pairs)


def other_core(a):
    return lax.ppermute(a, "c", [(0, 1), (1, 0)])


def call(body, outs, args, flops=0, scalars=1, **options):
    moved = sum(a.size * a.dtype.itemsize for a in (*args, *outs))
    single = len(outs) == 1
    return pl.pallas_call(
        body,
        out_shape=outs[0] if single else outs,
        in_specs=options.pop("in_specs", [SMEM] * scalars + [VMEM] * (len(args) - scalars)),
        out_specs=VMEM if single else [VMEM] * len(outs),
        compiler_params=pltpu.CompilerParams(vmem_limit_bytes=16 * 2**20),
        cost_estimate=pl.CostEstimate(flops=flops, bytes_accessed=moved, transcendentals=0),
        **options,
    )(*args)


def shaped(*shape, dtype=bf16):
    return jax.ShapeDtypeStruct(shape, dtype)


def take_rows(source, c, outs):
    n = outs[0].shape[1]
    count = outs[0].shape[0] * n
    span = NC * count
    per = n * len(outs) // NX
    i = lax.broadcasted_iota(i32, (count, span), 0)
    j = lax.broadcasted_iota(i32, (count, span), 1)
    wanted = (i // per % (n // per)) * (span * len(outs) // NX) + (i // n * NC + c) * per + i % per
    pick = (j == wanted).astype(bf16)
    for h, out in enumerate(outs):
        half = jnp.dot(
            pick, source[h * span:(h + 1) * span, :], preferred_element_type=f32
        ).astype(bf16)
        for p in range(out.shape[0]):
            out[p] = half[p * n:(p + 1) * n, :]


def own_rows_kernel(text, *outs):
    take_rows(text, 0, outs)


def core_rows_kernel(place, received, keep, send, *outs):
    @pl.when(place[3] == 0)
    def _():
        outs[0][...] = keep[...]
        outs[1][...] = send[...]

    @pl.when(place[3] != 0)
    def _():
        take_rows(received, 1, outs)


def flat_kernel(place, chunks, out):
    n = chunks.shape[1]
    per = n // 2

    def fill(core):
        for x in range(NX):
            for z in range(NZ):
                for s in range(STEPS):
                    held = s * (NX // STEPS)
                    if x >= NX // 2:
                        held = (held + (-1 if core else 1)) % NX
                    first = x % (NX // 2) * per
                    at = ((x * NZ + z) * STEPS + s) * per
                    out[at:at + per, :] = chunks[held * NZ + z, first:first + per, :]

    for core in range(NC):
        pl.when(place[3] == core)(functools.partial(fill, core))


def choose_kernel(place, keep, moved, out):
    owner = place[0] % (NX // STEPS) == 0

    @pl.when(owner)
    def _():
        out[...] = keep[...]

    @pl.when(jnp.logical_not(owner))
    def _():
        out[...] = moved[...]


def text_row(t, y, c, per):
    return t // per % STEPS, ((t // (STEPS * per) * NY + y) * NC + c) * per + t % per


def term_kernel(turns, place, factors, own, other, *refs):
    images, rest = refs[:len(turns)], refs[len(turns):]
    x, z, y, c = (place[n] for n in range(4))
    scale, bias = factors[0], factors[1]
    count = own.shape[0]
    per = count // (PLANE * STEPS)
    block = jnp.concatenate([own[...], other[...]], axis=0)
    t = lax.broadcasted_iota(i32, (NC * count, 1), 0)
    step, row = text_row(t % count, y, (c + t // count) % NC, per)
    kept = []
    for image, turn in zip(images, turns, strict=True):
        logits = scale * lax.dot_general(
            block, image[...], (((1,), (1,)), ((), ())), preferred_element_type=f32
        ) + bias
        held = (z == 0) & (c == 0) & ((y + turn) % NY == 0)
        mine = jnp.where(held & (step * (NX // STEPS) == x), row, -1)
        b = lax.broadcasted_iota(i32, logits.shape, 1)
        kept.append((jax.nn.sigmoid(logits) - (b == mine).astype(f32)).astype(bf16))
    total = None
    for weights, image in zip(kept, images, strict=True):
        term = jnp.dot(weights, image[...], preferred_element_type=f32)
        total = term if total is None else total + term
    rest[0][...] = total[:count]
    rest[1][...] = total[count:].astype(bf16)


def add_kernel(mine, received, out):
    n = out.shape[1]
    total = (mine[...] + received[...].astype(f32)).astype(bf16)
    for p in range(out.shape[0]):
        out[p] = total[p * n:(p + 1) * n, :]


def sum_kernel(factors, terms, out):
    total = terms[0].astype(f32)
    for p in range(1, terms.shape[0]):
        total = total + terms[p].astype(f32)
    total = factors[0] * total
    per = out.shape[1]
    for s in range(STEPS):
        out[s] = total[s * per:(s + 1) * per, :]


def image_kernel(offsets, place, factors, image, *refs):
    *texts, grad, loss, block = refs
    x, z, y, c = (place[n] for n in range(4))
    scale, bias = factors[0], factors[1]
    rows = image.shape[0]
    count = texts[0].shape[0]
    per = count // (PLANE * STEPS)
    held = (z == 0) & (y == 0) & (c == 0)
    t = lax.broadcasted_iota(i32, (1, count), 1)
    wanted = []
    for n, (text, (turn, dc)) in enumerate(zip(texts, offsets, strict=True)):
        dy = turn * (2 * c - 1)
        block[n * count:(n + 1) * count, :] = text[...]
        step, row = text_row(t, (y + dy + NY) % NY, (c + dc) % NC, per)
        wanted.append(jnp.where(held & (step * (NX // STEPS) == x), row, -1))
    row = jnp.concatenate(wanted, axis=1)

    def fill(with_positives):
        logits = scale * lax.dot_general(
            image[...], block[...], (((1,), (1,)), ((), ())), preferred_element_type=f32
        ) + bias
        e = jnp.exp(jnp.minimum(logits, -logits))
        u = 1.0 + e
        near = pl.reciprocal(u, approx=True)
        r = near * (2.0 - u * near)
        sigmoid = jnp.where(logits >= 0, r, e * r)
        above = jnp.maximum(logits, 0.0)
        if with_positives:
            positive = lax.broadcasted_iota(i32, logits.shape, 0) == row
            above = above - jnp.where(positive, logits, 0.0)
            sigmoid = sigmoid - positive.astype(f32)
        s = e
        while s.shape[1] > 128:
            half = s.shape[1] // 2
            s = s[:, :half] + s[:, half:] + s[:, :half] * s[:, half:]
            above = above[:, :half] + above[:, half:]
        u = 1.0 + s
        log1p = jnp.log(u) + (s - (u - 1.0)) / u
        loss[...] = jnp.sum(above + log1p, axis=1)
        grad[...] = scale * jnp.dot(
            sigmoid.astype(bf16), block[...], preferred_element_type=f32
        )

    pl.when(held)(lambda: fill(True))
    pl.when(jnp.logical_not(held))(lambda: fill(False))


def local(image, text, log_scale, logit_bias):
    rows, width = image.shape
    place = jnp.stack([lax.axis_index(a) for a in AXES]).astype(i32)
    factors = jnp.concatenate([jnp.exp(log_scale), logit_bias])
    per = rows // (PLANE * NY * NC)
    count = PLANE * STEPS * per

    chunk = shaped(NZ * NY, STEPS * per, width)
    received = lax.ppermute(text, "c", [(0, 1)])
    own = call(own_rows_kernel, [chunk] * 2, (text,), scalars=0)
    keep, send = call(core_rows_kernel, [chunk] * 2, (place, received, *own))
    owners = range(0, NX, NX // STEPS)
    pairs = [
        (device(x, 0, 0, c), device((x + 1 - 2 * c) % NX, 0, 0, c)) for x in owners for c in range(NC)
    ]
    moved = lax.ppermute(send, AXES, pairs)
    joined = call(choose_kernel, [chunk], (place, keep, moved))

    images = [image, around(image, 1)]
    again, images[1] = lax.optimization_barrier((image, images[1]))
    images += [around(again, -1), around(images[1], 1)]

    spread = lax.all_to_all(joined, ("z", "y"), 0, 0, tiled=True)
    everywhere = jnp.broadcast_to(spread[:1], (PLANE, STEPS * per, width))
    everywhere, images[1] = lax.optimization_barrier((everywhere, images[1]))
    chunks = lax.all_to_all(everywhere, ("x", "z"), 0, 0, tiled=True)
    texts = call(
        flat_kernel,
        [shaped(count, width)],
        (place, chunks),
    )

    other = other_core(texts)
    turns = (0, 1, NY - 1, 2)
    flops = 4 * rows * NC * count * width
    mine, theirs = call(
        functools.partial(term_kernel, turns),
        [shaped(count, width, dtype=f32), shaped(count, width)],
        (place, factors, texts, other, *images),
        flops=4 * flops,
        scalars=2,
    )
    line = [texts, around(texts, 1), around(texts, -1)]
    line.append(around(line[1], 1))
    passed = other_core(theirs)
    passed, line[1], line[2] = lax.optimization_barrier((passed, line[1], line[2]))
    term = call(add_kernel, [shaped(PLANE, STEPS * per, width)], (mine, passed), scalars=0)
    terms = lax.all_to_all(term, ("x", "z"), 0, 0, tiled=True)
    text_grad = call(sum_kernel, [shaped(STEPS, per, width, dtype=f32)], (factors, terms))

    across = [other] + [other_core(a) for a in line[1:]]
    offsets = [(0, 0), (-1, 0), (1, 0), (2, 0), (0, 1), (1, 1), (-1, 1), (2, 1)]
    image_grad, row_loss = call(
        functools.partial(image_kernel, offsets),
        [shaped(rows, width, dtype=f32), shaped(rows, dtype=f32)],
        (place, factors, image, *line, *across),
        flops=NY * flops,
        scalars=2,
        scratch_shapes=[pltpu.VMEM((len(offsets) * count, width), bf16)],
    )
    return image_grad, text_grad, row_loss


def solution(mesh):
    mesh = Mesh(mesh.devices.reshape(NX, NZ, NY, NC), AXES)
    in_specs = (P(AXES, None), P(AXES, None), P(), P())
    out_specs = (P(AXES, None), P(None, AXES, None), P(AXES))
    return jax.shard_map(local, mesh=mesh, in_specs=in_specs, out_specs=out_specs, check_vma=False)
```

```python
import functools

import jax
import jax.numpy as jnp
from jax import lax
from jax.experimental import pallas as pl
from jax.experimental.pallas import tpu as pltpu
from jax.sharding import Mesh, PartitionSpec as P

STEPS = 2
NX, NZ, NY, NC = 4, 8, 4, 2
AXES = ("x", "z", "y", "c")
PLANE = NX * NZ
f32, bf16, i32 = jnp.float32, jnp.bfloat16, jnp.int32
VMEM = pl.BlockSpec(memory_space=pltpu.VMEM)
SMEM = pl.BlockSpec(memory_space=pltpu.SMEM)


def device(x, z, y, c):
    return ((x * NZ + z) * NY + y) * NC + c


def around(a, way):
    pairs = [
        (y * NC + c, (y + way * (2 * c - 1)) % NY * NC + c) for y in range(NY) for c in range(NC)
    ]
    return lax.ppermute(a, ("y", "c"), pairs)


def other_core(a):
    return lax.ppermute(a, "c", [(0, 1), (1, 0)])


def call(body, outs, args, flops=0, scalars=1, **options):
    moved = sum(a.size * a.dtype.itemsize for a in (*args, *outs))
    single = len(outs) == 1
    return pl.pallas_call(
        body,
        out_shape=outs[0] if single else outs,
        in_specs=options.pop("in_specs", [SMEM] * scalars + [VMEM] * (len(args) - scalars)),
        out_specs=VMEM if single else [VMEM] * len(outs),
        compiler_params=pltpu.CompilerParams(vmem_limit_bytes=16 * 2**20),
        cost_estimate=pl.CostEstimate(flops=flops, bytes_accessed=moved, transcendentals=0),
        **options,
    )(*args)


def shaped(*shape, dtype=bf16):
    return jax.ShapeDtypeStruct(shape, dtype)


def take_rows(source, c, outs):
    n = outs[0].shape[1]
    count = outs[0].shape[0] * n
    span = NC * count
    per = n * len(outs) // NX
    i = lax.broadcasted_iota(i32, (count, span), 0)
    j = lax.broadcasted_iota(i32, (count, span), 1)
    wanted = (i // per % (n // per)) * (span * len(outs) // NX) + (i // n * NC + c) * per + i % per
    pick = (j == wanted).astype(bf16)
    for h, out in enumerate(outs):
        half = jnp.dot(
            pick, source[h * span:(h + 1) * span, :], preferred_element_type=f32
        ).astype(bf16)
        for p in range(out.shape[0]):
            out[p] = half[p * n:(p + 1) * n, :]


def own_rows_kernel(text, *outs):
    take_rows(text, 0, outs)


def core_rows_kernel(place, received, keep, send, *outs):
    @pl.when(place[3] == 0)
    def _():
        outs[0][...] = keep[...]
        outs[1][...] = send[...]

    @pl.when(place[3] != 0)
    def _():
        take_rows(received, 1, outs)


def flat_kernel(place, chunks, out):
    n = chunks.shape[1]
    per = n // 2

    def fill(core):
        for x in range(NX):
            for z in range(NZ):
                for s in range(STEPS):
                    held = s * (NX // STEPS)
                    if x >= NX // 2:
                        held = (held + (1 if core else -1)) % NX
                    first = x % (NX // 2) * per
                    at = ((x * NZ + z) * STEPS + s) * per
                    out[at:at + per, :] = chunks[held * NZ + z, first:first + per, :]

    for core in range(NC):
        pl.when(place[3] == core)(functools.partial(fill, core))


def choose_kernel(place, keep, moved, out):
    owner = place[0] % (NX // STEPS) == 0

    @pl.when(owner)
    def _():
        out[...] = keep[...]

    @pl.when(jnp.logical_not(owner))
    def _():
        out[...] = moved[...]


def text_row(t, y, c, per):
    return t // per % STEPS, ((t // (STEPS * per) * NY + y) * NC + c) * per + t % per


def term_kernel(turns, place, factors, own, other, *refs):
    images, rest = refs[:len(turns)], refs[len(turns):]
    x, z, y, c = (place[n] for n in range(4))
    scale, bias = factors[0], factors[1]
    count = own.shape[0]
    per = count // (PLANE * STEPS)
    block = jnp.concatenate([own[...], other[...]], axis=0)
    t = lax.broadcasted_iota(i32, (NC * count, 1), 0)
    step, row = text_row(t % count, y, (c + t // count) % NC, per)
    kept = []
    for image, turn in zip(images, turns, strict=True):
        logits = scale * lax.dot_general(
            block, image[...], (((1,), (1,)), ((), ())), preferred_element_type=f32
        ) + bias
        held = (z == 0) & (c == 0) & ((y + turn) % NY == 0)
        mine = jnp.where(held & (step * (NX // STEPS) == x), row, -1)
        b = lax.broadcasted_iota(i32, logits.shape, 1)
        kept.append((jax.nn.sigmoid(logits) - (b == mine).astype(f32)).astype(bf16))
    total = None
    for weights, image in zip(kept, images, strict=True):
        term = jnp.dot(weights, image[...], preferred_element_type=f32)
        total = term if total is None else total + term
    rest[0][...] = total[:count]
    rest[1][...] = total[count:].astype(bf16)


def add_kernel(mine, received, out):
    n = out.shape[1]
    total = (mine[...] + received[...].astype(f32)).astype(bf16)
    for p in range(out.shape[0]):
        out[p] = total[p * n:(p + 1) * n, :]


def sum_kernel(factors, terms, out):
    total = terms[0].astype(f32)
    for p in range(1, terms.shape[0]):
        total = total + terms[p].astype(f32)
    total = factors[0] * total
    per = out.shape[1]
    for s in range(STEPS):
        out[s] = total[s * per:(s + 1) * per, :]


def image_kernel(offsets, place, factors, image, *refs):
    *texts, grad, loss, block = refs
    x, z, y, c = (place[n] for n in range(4))
    scale, bias = factors[0], factors[1]
    rows = image.shape[0]
    count = texts[0].shape[0]
    per = count // (PLANE * STEPS)
    held = (z == 0) & (y == 0) & (c == 0)
    t = lax.broadcasted_iota(i32, (1, count), 1)
    wanted = []
    for n, (text, (turn, dc)) in enumerate(zip(texts, offsets, strict=True)):
        dy = turn * (2 * c - 1)
        block[n * count:(n + 1) * count, :] = text[...]
        step, row = text_row(t, (y + dy + NY) % NY, (c + dc) % NC, per)
        wanted.append(jnp.where(held & (step * (NX // STEPS) == x), row, -1))
    row = jnp.concatenate(wanted, axis=1)

    def fill(with_positives):
        logits = scale * lax.dot_general(
            image[...], block[...], (((1,), (1,)), ((), ())), preferred_element_type=f32
        ) + bias
        e = jnp.exp(jnp.minimum(logits, -logits))
        u = 1.0 + e
        near = pl.reciprocal(u, approx=True)
        r = near * (2.0 - u * near)
        sigmoid = jnp.where(logits >= 0, r, e * r)
        above = jnp.maximum(logits, 0.0)
        if with_positives:
            positive = lax.broadcasted_iota(i32, logits.shape, 0) == row
            above = above - jnp.where(positive, logits, 0.0)
            sigmoid = sigmoid - positive.astype(f32)
        s = e
        while s.shape[1] > 128:
            half = s.shape[1] // 2
            s = s[:, :half] + s[:, half:] + s[:, :half] * s[:, half:]
            above = above[:, :half] + above[:, half:]
        u = 1.0 + s
        log1p = jnp.log(u) + (s - (u - 1.0)) / u
        loss[...] = jnp.sum(above + log1p, axis=1)
        grad[...] = scale * jnp.dot(
            sigmoid.astype(bf16), block[...], preferred_element_type=f32
        )

    pl.when(held)(lambda: fill(True))
    pl.when(jnp.logical_not(held))(lambda: fill(False))


def local(image, text, log_scale, logit_bias):
    rows, width = image.shape
    place = jnp.stack([lax.axis_index(a) for a in AXES]).astype(i32)
    factors = jnp.concatenate([jnp.exp(log_scale), logit_bias])
    per = rows // (PLANE * NY * NC)
    count = PLANE * STEPS * per

    chunk = shaped(NZ * NY, STEPS * per, width)
    received = lax.ppermute(text, "c", [(0, 1)])
    own = call(own_rows_kernel, [chunk] * 2, (text,), scalars=0)
    keep, send = call(core_rows_kernel, [chunk] * 2, (place, received, *own))
    owners = range(0, NX, NX // STEPS)
    pairs = [
        (device(x, 0, 0, c), device((x - 1 + 2 * c) % NX, 0, 0, c)) for x in owners for c in range(NC)
    ]
    moved = lax.ppermute(send, AXES, pairs)
    joined = call(choose_kernel, [chunk], (place, keep, moved))

    images = [image, around(image, 1)]
    again, images[1] = lax.optimization_barrier((image, images[1]))
    images += [around(again, -1), around(images[1], 1)]

    spread = lax.all_to_all(joined, ("z", "y"), 0, 0, tiled=True)
    everywhere = jnp.broadcast_to(spread[:1], (PLANE, STEPS * per, width))
    everywhere, images[1] = lax.optimization_barrier((everywhere, images[1]))
    chunks = lax.all_to_all(everywhere, ("x", "z"), 0, 0, tiled=True)
    texts = call(
        flat_kernel,
        [shaped(count, width)],
        (place, chunks),
    )

    other = other_core(texts)
    turns = (0, 1, NY - 1, 2)
    flops = 4 * rows * NC * count * width
    mine, theirs = call(
        functools.partial(term_kernel, turns),
        [shaped(count, width, dtype=f32), shaped(count, width)],
        (place, factors, texts, other, *images),
        flops=4 * flops,
        scalars=2,
    )
    line = [texts, around(texts, 1), around(texts, -1)]
    line.append(around(line[1], 1))
    passed = other_core(theirs)
    passed, line[1], line[2] = lax.optimization_barrier((passed, line[1], line[2]))
    term = call(add_kernel, [shaped(PLANE, STEPS * per, width)], (mine, passed), scalars=0)
    terms = lax.all_to_all(term, ("x", "z"), 0, 0, tiled=True)
    text_grad = call(sum_kernel, [shaped(STEPS, per, width, dtype=f32)], (factors, terms))

    across = [other] + [other_core(a) for a in line[1:]]
    offsets = [(0, 0), (-1, 0), (1, 0), (2, 0), (0, 1), (1, 1), (-1, 1), (2, 1)]
    image_grad, row_loss = call(
        functools.partial(image_kernel, offsets),
        [shaped(rows, width, dtype=f32), shaped(rows, dtype=f32)],
        (place, factors, image, *line, *across),
        flops=NY * flops,
        scalars=2,
        scratch_shapes=[pltpu.VMEM((len(offsets) * count, width), bf16)],
    )
    return image_grad, text_grad, row_loss


def solution(mesh):
    mesh = Mesh(mesh.devices.reshape(NX, NZ, NY, NC), AXES)
    in_specs = (P(AXES, None), P(AXES, None), P(), P())
    out_specs = (P(AXES, None), P(None, AXES, None), P(AXES))
    return jax.shard_map(local, mesh=mesh, in_specs=in_specs, out_specs=out_specs, check_vma=False)
```

```python
import functools

import jax
import jax.numpy as jnp
from jax import lax
from jax.experimental import pallas as pl
from jax.experimental.pallas import tpu as pltpu
from jax.sharding import Mesh, PartitionSpec as P

STEPS = 2
NX, NZ, NY, NC = 4, 8, 4, 2
AXES = ("x", "z", "y", "c")
PLANE = NX * NZ
f32, bf16, i32 = jnp.float32, jnp.bfloat16, jnp.int32
VMEM = pl.BlockSpec(memory_space=pltpu.VMEM)
SMEM = pl.BlockSpec(memory_space=pltpu.SMEM)


def device(x, z, y, c):
    return ((x * NZ + z) * NY + y) * NC + c


def around(a, way):
    pairs = [
        (y * NC + c, (y + way * (2 * c - 1)) % NY * NC + c) for y in range(NY) for c in range(NC)
    ]
    return lax.ppermute(a, ("y", "c"), pairs)


def other_core(a):
    return lax.ppermute(a, "c", [(0, 1), (1, 0)])


def call(body, outs, args, flops=0, scalars=1, **options):
    moved = sum(a.size * a.dtype.itemsize for a in (*args, *outs))
    single = len(outs) == 1
    return pl.pallas_call(
        body,
        out_shape=outs[0] if single else outs,
        in_specs=options.pop("in_specs", [SMEM] * scalars + [VMEM] * (len(args) - scalars)),
        out_specs=VMEM if single else [VMEM] * len(outs),
        compiler_params=pltpu.CompilerParams(vmem_limit_bytes=16 * 2**20),
        cost_estimate=pl.CostEstimate(flops=flops, bytes_accessed=moved, transcendentals=0),
        **options,
    )(*args)


def shaped(*shape, dtype=bf16):
    return jax.ShapeDtypeStruct(shape, dtype)


def take_rows(source, c, outs):
    n = outs[0].shape[1]
    count = outs[0].shape[0] * n
    span = NC * count
    per = n * len(outs) // NX
    i = lax.broadcasted_iota(i32, (count, span), 0)
    j = lax.broadcasted_iota(i32, (count, span), 1)
    wanted = (i // per % (n // per)) * (span * len(outs) // NX) + (i // n * NC + c) * per + i % per
    pick = (j == wanted).astype(bf16)
    for h, out in enumerate(outs):
        half = jnp.dot(
            pick, source[h * span:(h + 1) * span, :], preferred_element_type=f32
        ).astype(bf16)
        for p in range(out.shape[0]):
            out[p] = half[p * n:(p + 1) * n, :]


def own_rows_kernel(text, *outs):
    take_rows(text, 0, outs)


def core_rows_kernel(place, received, keep, send, *outs):
    @pl.when(place[3] == 0)
    def _():
        outs[0][...] = keep[...]
        outs[1][...] = send[...]

    @pl.when(place[3] != 0)
    def _():
        take_rows(received, 1, outs)


def flat_kernel(place, chunks, out):
    n = chunks.shape[1]
    per = n // 2

    def fill(core):
        for x in range(NX):
            for z in range(NZ):
                for s in range(STEPS):
                    held = s * (NX // STEPS)
                    if x >= NX // 2:
                        held = (held + (1 if core else -1)) % NX
                    first = x % (NX // 2) * per
                    at = ((x * NZ + z) * STEPS + s) * per
                    out[at:at + per, :] = chunks[held * NZ + z, first:first + per, :]

    for core in range(NC):
        pl.when(place[3] == core)(functools.partial(fill, core))


def choose_kernel(place, keep, moved, out):
    owner = place[0] % (NX // STEPS) == 0

    @pl.when(owner)
    def _():
        out[...] = keep[...]

    @pl.when(jnp.logical_not(owner))
    def _():
        out[...] = moved[...]


def text_row(t, y, c, per):
    return t // per % STEPS, ((t // (STEPS * per) * NY + y) * NC + c) * per + t % per


def term_kernel(turns, place, factors, own, other, *refs):
    images, rest = refs[:len(turns)], refs[len(turns):]
    x, z, y, c = (place[n] for n in range(4))
    scale, bias = factors[0], factors[1]
    count = own.shape[0]
    per = count // (PLANE * STEPS)
    block = jnp.concatenate([own[...], other[...]], axis=0)
    t = lax.broadcasted_iota(i32, (NC * count, 1), 0)
    step, row = text_row(t % count, y, (c + t // count) % NC, per)
    kept = []
    for image, turn in zip(images, turns, strict=True):
        logits = scale * lax.dot_general(
            block, image[...], (((1,), (1,)), ((), ())), preferred_element_type=f32
        ) + bias
        held = (z == 0) & (c == 0) & ((y + turn) % NY == 0)
        mine = jnp.where(held & (step * (NX // STEPS) == x), row, -1)
        b = lax.broadcasted_iota(i32, logits.shape, 1)
        e = jnp.exp(jnp.minimum(logits, -logits))
        near = pl.reciprocal(1.0 + e, approx=True)
        r = near * (2.0 - (1.0 + e) * near)
        sigmoid = jnp.where(logits >= 0, r, e * r)
        kept.append((sigmoid - (b == mine).astype(f32)).astype(bf16))
    total = None
    for weights, image in zip(kept, images, strict=True):
        term = jnp.dot(weights, image[...], preferred_element_type=f32)
        total = term if total is None else total + term
    rest[0][...] = total[:count]
    rest[1][...] = total[count:].astype(bf16)


def add_kernel(mine, received, out):
    n = out.shape[1]
    total = (mine[...] + received[...].astype(f32)).astype(bf16)
    for p in range(out.shape[0]):
        out[p] = total[p * n:(p + 1) * n, :]


def sum_kernel(factors, terms, out):
    total = terms[0].astype(f32)
    for p in range(1, terms.shape[0]):
        total = total + terms[p].astype(f32)
    total = factors[0] * total
    per = out.shape[1]
    for s in range(STEPS):
        out[s] = total[s * per:(s + 1) * per, :]


def image_kernel(offsets, place, factors, image, *refs):
    *texts, grad, loss, block = refs
    x, z, y, c = (place[n] for n in range(4))
    scale, bias = factors[0], factors[1]
    rows = image.shape[0]
    count = texts[0].shape[0]
    per = count // (PLANE * STEPS)
    held = (z == 0) & (y == 0) & (c == 0)
    t = lax.broadcasted_iota(i32, (1, count), 1)
    wanted = []
    for n, (text, (turn, dc)) in enumerate(zip(texts, offsets, strict=True)):
        dy = turn * (2 * c - 1)
        block[n * count:(n + 1) * count, :] = text[...]
        step, row = text_row(t, (y + dy + NY) % NY, (c + dc) % NC, per)
        wanted.append(jnp.where(held & (step * (NX // STEPS) == x), row, -1))
    row = jnp.concatenate(wanted, axis=1)

    def fill(with_positives):
        logits = scale * lax.dot_general(
            image[...], block[...], (((1,), (1,)), ((), ())), preferred_element_type=f32
        ) + bias
        e = jnp.exp(jnp.minimum(logits, -logits))
        u = 1.0 + e
        near = pl.reciprocal(u, approx=True)
        r = near * (2.0 - u * near)
        sigmoid = jnp.where(logits >= 0, r, e * r)
        above = jnp.maximum(logits, 0.0)
        if with_positives:
            positive = lax.broadcasted_iota(i32, logits.shape, 0) == row
            above = above - jnp.where(positive, logits, 0.0)
            sigmoid = sigmoid - positive.astype(f32)
        s = e
        while s.shape[1] > 128:
            half = s.shape[1] // 2
            s = s[:, :half] + s[:, half:] + s[:, :half] * s[:, half:]
            above = above[:, :half] + above[:, half:]
        u = 1.0 + s
        log1p = jnp.log(u) + (s - (u - 1.0)) / u
        loss[...] = jnp.sum(above + log1p, axis=1)
        grad[...] = scale * jnp.dot(
            sigmoid.astype(bf16), block[...], preferred_element_type=f32
        )

    pl.when(held)(lambda: fill(True))
    pl.when(jnp.logical_not(held))(lambda: fill(False))


def local(image, text, log_scale, logit_bias):
    rows, width = image.shape
    place = jnp.stack([lax.axis_index(a) for a in AXES]).astype(i32)
    factors = jnp.concatenate([jnp.exp(log_scale), logit_bias])
    per = rows // (PLANE * NY * NC)
    count = PLANE * STEPS * per

    chunk = shaped(NZ * NY, STEPS * per, width)
    owners = range(0, NX, NX // STEPS)
    received = lax.ppermute(
        text, AXES, [(device(x, 0, 0, 0), device(x, 0, 0, 1)) for x in owners]
    )
    own = call(own_rows_kernel, [chunk] * 2, (text,), scalars=0)
    keep, send = call(core_rows_kernel, [chunk] * 2, (place, received, *own))
    pairs = [
        (device(x, 0, 0, c), device((x - 1 + 2 * c) % NX, 0, 0, c)) for x in owners for c in range(NC)
    ]
    moved = lax.ppermute(send, AXES, pairs)
    joined = call(choose_kernel, [chunk], (place, keep, moved))

    images = [image, around(image, 1)]
    again, images[1] = lax.optimization_barrier((image, images[1]))
    images += [around(again, -1), around(images[1], 1)]

    spread = lax.all_to_all(joined, ("z", "y"), 0, 0, tiled=True)
    everywhere = jnp.broadcast_to(spread[:1], (PLANE, STEPS * per, width))
    everywhere, images[1] = lax.optimization_barrier((everywhere, images[1]))
    chunks = lax.all_to_all(everywhere, ("x", "z"), 0, 0, tiled=True)
    texts = call(
        flat_kernel,
        [shaped(count, width)],
        (place, chunks),
    )

    other = other_core(texts)
    turns = (0, 1, NY - 1, 2)
    flops = 4 * rows * NC * count * width
    mine, theirs = call(
        functools.partial(term_kernel, turns),
        [shaped(count, width, dtype=f32), shaped(count, width)],
        (place, factors, texts, other, *images),
        flops=4 * flops,
        scalars=2,
    )
    line = [texts, around(texts, 1), around(texts, -1)]
    line.append(around(line[1], 1))
    passed = other_core(theirs)
    passed, line[1], line[2] = lax.optimization_barrier((passed, line[1], line[2]))
    term = call(add_kernel, [shaped(PLANE, STEPS * per, width)], (mine, passed), scalars=0)
    terms = lax.all_to_all(term, ("x", "z"), 0, 0, tiled=True)
    text_grad = call(sum_kernel, [shaped(STEPS, per, width, dtype=f32)], (factors, terms))

    across = [other] + [other_core(a) for a in line[1:]]
    offsets = [(0, 0), (-1, 0), (1, 0), (2, 0), (0, 1), (1, 1), (-1, 1), (2, 1)]
    image_grad, row_loss = call(
        functools.partial(image_kernel, offsets),
        [shaped(rows, width, dtype=f32), shaped(rows, dtype=f32)],
        (place, factors, image, *line, *across),
        flops=NY * flops,
        scalars=2,
        scratch_shapes=[pltpu.VMEM((len(offsets) * count, width), bf16)],
    )
    return image_grad, text_grad, row_loss


def solution(mesh):
    mesh = Mesh(mesh.devices.reshape(NX, NZ, NY, NC), AXES)
    in_specs = (P(AXES, None), P(AXES, None), P(), P())
    out_specs = (P(AXES, None), P(None, AXES, None), P(AXES))
    return jax.shard_map(local, mesh=mesh, in_specs=in_specs, out_specs=out_specs, check_vma=False)
```

```python
import functools

import jax
import jax.numpy as jnp
from jax import lax
from jax.experimental import pallas as pl
from jax.experimental.pallas import tpu as pltpu
from jax.sharding import Mesh, PartitionSpec as P

STEPS = 2
NX, NZ, NY, NC = 4, 8, 4, 2
AXES = ("x", "z", "y", "c")
PLANE = NX * NZ
f32, bf16, i32 = jnp.float32, jnp.bfloat16, jnp.int32
VMEM = pl.BlockSpec(memory_space=pltpu.VMEM)
SMEM = pl.BlockSpec(memory_space=pltpu.SMEM)


def device(x, z, y, c):
    return ((x * NZ + z) * NY + y) * NC + c


def around(a, way):
    pairs = [
        (y * NC + c, (y + way * (2 * c - 1)) % NY * NC + c) for y in range(NY) for c in range(NC)
    ]
    return lax.ppermute(a, ("y", "c"), pairs)


def other_core(a):
    return lax.ppermute(a, "c", [(0, 1), (1, 0)])


def call(body, outs, args, flops=0, scalars=1, **options):
    moved = sum(a.size * a.dtype.itemsize for a in (*args, *outs))
    single = len(outs) == 1
    return pl.pallas_call(
        body,
        out_shape=outs[0] if single else outs,
        in_specs=options.pop("in_specs", [SMEM] * scalars + [VMEM] * (len(args) - scalars)),
        out_specs=VMEM if single else [VMEM] * len(outs),
        compiler_params=pltpu.CompilerParams(vmem_limit_bytes=16 * 2**20),
        cost_estimate=pl.CostEstimate(flops=flops, bytes_accessed=moved, transcendentals=0),
        **options,
    )(*args)


def shaped(*shape, dtype=bf16):
    return jax.ShapeDtypeStruct(shape, dtype)


def take_rows(source, c, outs):
    n = outs[0].shape[1]
    count = outs[0].shape[0] * n
    span = NC * count
    per = n * len(outs) // NX
    i = lax.broadcasted_iota(i32, (count, span), 0)
    j = lax.broadcasted_iota(i32, (count, span), 1)
    wanted = (i // per % (n // per)) * (span * len(outs) // NX) + (i // n * NC + c) * per + i % per
    pick = (j == wanted).astype(bf16)
    for h, out in enumerate(outs):
        half = jnp.dot(
            pick, source[h * span:(h + 1) * span, :], preferred_element_type=f32
        ).astype(bf16)
        for p in range(out.shape[0]):
            out[p] = half[p * n:(p + 1) * n, :]


def own_rows_kernel(text, *outs):
    take_rows(text, 0, outs)


def core_rows_kernel(place, received, keep, send, *outs):
    @pl.when(place[3] == 0)
    def _():
        outs[0][...] = keep[...]
        outs[1][...] = send[...]

    @pl.when(place[3] != 0)
    def _():
        take_rows(received, 1, outs)


def flat_kernel(place, chunks, out):
    n = chunks.shape[1]
    per = n // 2

    def fill(core):
        for x in range(NX):
            for z in range(NZ):
                for s in range(STEPS):
                    held = s * (NX // STEPS)
                    if x >= NX // 2:
                        held = (held + (1 if core else -1)) % NX
                    first = x % (NX // 2) * per
                    at = ((x * NZ + z) * STEPS + s) * per
                    out[at:at + per, :] = chunks[held * NZ + z, first:first + per, :]

    for core in range(NC):
        pl.when(place[3] == core)(functools.partial(fill, core))


def choose_kernel(place, keep, moved, out):
    owner = place[0] % (NX // STEPS) == 0

    @pl.when(owner)
    def _():
        out[...] = keep[...]

    @pl.when(jnp.logical_not(owner))
    def _():
        out[...] = moved[...]


def text_row(t, y, c, per):
    return t // per % STEPS, ((t // (STEPS * per) * NY + y) * NC + c) * per + t % per


def term_kernel(turns, place, factors, own, other, *refs):
    images, rest = refs[:len(turns)], refs[len(turns):]
    x, z, y, c = (place[n] for n in range(4))
    scale, bias = factors[0], factors[1]
    count = own.shape[0]
    per = count // (PLANE * STEPS)
    block = jnp.concatenate([own[...], other[...]], axis=0)
    t = lax.broadcasted_iota(i32, (NC * count, 1), 0)
    step, row = text_row(t % count, y, (c + t // count) % NC, per)
    kept = []
    for image, turn in zip(images, turns, strict=True):
        logits = scale * lax.dot_general(
            block, image[...], (((1,), (1,)), ((), ())), preferred_element_type=f32
        ) + bias
        held = (z == 0) & (c == 0) & ((y + turn) % NY == 0)
        mine = jnp.where(held & (step * (NX // STEPS) == x), row, -1)
        b = lax.broadcasted_iota(i32, logits.shape, 1)
        e = jnp.exp(jnp.minimum(logits, -logits))
        near = pl.reciprocal(1.0 + e, approx=True)
        r = near * (2.0 - (1.0 + e) * near)
        sigmoid = jnp.where(logits >= 0, r, e * r)
        kept.append((sigmoid - (b == mine).astype(f32)).astype(bf16))
    total = None
    for weights, image in zip(kept, images, strict=True):
        term = jnp.dot(weights, image[...], preferred_element_type=f32)
        total = term if total is None else total + term
    rest[0][...] = total[:count]
    rest[1][...] = total[count:].astype(bf16)


def add_kernel(mine, received, out):
    n = out.shape[1]
    total = (mine[...] + received[...].astype(f32)).astype(bf16)
    for p in range(out.shape[0]):
        out[p] = total[p * n:(p + 1) * n, :]


def sum_kernel(factors, terms, out):
    total = terms[0].astype(f32)
    for p in range(1, terms.shape[0]):
        total = total + terms[p].astype(f32)
    total = factors[0] * total
    per = out.shape[1]
    for s in range(STEPS):
        out[s] = total[s * per:(s + 1) * per, :]


def image_kernel(offsets, place, factors, image, *refs):
    *texts, grad, loss, block = refs
    x, z, y, c = (place[n] for n in range(4))
    scale, bias = factors[0], factors[1]
    rows = image.shape[0]
    count = texts[0].shape[0]
    per = count // (PLANE * STEPS)
    held = (z == 0) & (y == 0) & (c == 0)
    t = lax.broadcasted_iota(i32, (1, count), 1)
    wanted = []
    for n, (text, (turn, dc)) in enumerate(zip(texts, offsets, strict=True)):
        dy = turn * (2 * c - 1)
        block[n * count:(n + 1) * count, :] = text[...]
        step, row = text_row(t, (y + dy + NY) % NY, (c + dc) % NC, per)
        wanted.append(jnp.where(held & (step * (NX // STEPS) == x), row, -1))
    row = jnp.concatenate(wanted, axis=1)

    def fill(with_positives):
        logits = scale * lax.dot_general(
            image[...], block[...], (((1,), (1,)), ((), ())), preferred_element_type=f32
        ) + bias
        e = jnp.exp(jnp.minimum(logits, -logits))
        u = 1.0 + e
        near = pl.reciprocal(u, approx=True)
        r = near * (2.0 - u * near)
        sigmoid = jnp.where(logits >= 0, r, e * r)
        above = jnp.maximum(logits, 0.0)
        if with_positives:
            positive = lax.broadcasted_iota(i32, logits.shape, 0) == row
            above = above - jnp.where(positive, logits, 0.0)
            sigmoid = sigmoid - positive.astype(f32)
        s = e
        while s.shape[1] > 128:
            half = s.shape[1] // 2
            s = s[:, :half] + s[:, half:] + s[:, :half] * s[:, half:]
            above = above[:, :half] + above[:, half:]
        u = 1.0 + s
        log1p = jnp.log(u) + (s - (u - 1.0)) / u
        loss[...] = jnp.sum(above + log1p, axis=1)
        grad[...] = scale * jnp.dot(
            sigmoid.astype(bf16), block[...], preferred_element_type=f32
        )

    pl.when(held)(lambda: fill(True))
    pl.when(jnp.logical_not(held))(lambda: fill(False))


def local(image, text, log_scale, logit_bias):
    rows, width = image.shape
    place = jnp.stack([lax.axis_index(a) for a in AXES]).astype(i32)
    factors = jnp.concatenate([jnp.exp(log_scale), logit_bias])
    per = rows // (PLANE * NY * NC)
    count = PLANE * STEPS * per

    chunk = shaped(NZ * NY, STEPS * per, width)
    owners = range(0, NX, NX // STEPS)
    received = lax.ppermute(
        text, AXES, [(device(x, 0, 0, 0), device(x, 0, 0, 1)) for x in owners]
    )
    own = call(own_rows_kernel, [chunk] * 2, (text,), scalars=0)
    keep, send = call(core_rows_kernel, [chunk] * 2, (place, received, *own))
    pairs = [
        (device(x, 0, 0, c), device((x - 1 + 2 * c) % NX, 0, 0, c)) for x in owners for c in range(NC)
    ]
    moved = lax.ppermute(send, AXES, pairs)
    joined = call(choose_kernel, [chunk], (place, keep, moved))

    images = [image, around(image, 1)]
    again, images[1] = lax.optimization_barrier((image, images[1]))
    images += [around(again, -1), around(images[1], 1)]

    spread = lax.all_to_all(joined, ("z", "y"), 0, 0, tiled=True)
    everywhere = jnp.broadcast_to(spread[:1], (PLANE, STEPS * per, width))
    everywhere, images[1] = lax.optimization_barrier((everywhere, images[1]))
    chunks = lax.all_to_all(everywhere, ("x", "z"), 0, 0, tiled=True)
    texts = call(
        flat_kernel,
        [shaped(count, width)],
        (place, chunks),
    )

    other = other_core(texts)
    turns = (0, 1, NY - 1, 2)
    flops = 4 * rows * NC * count * width
    mine, theirs = call(
        functools.partial(term_kernel, turns),
        [shaped(count, width, dtype=f32), shaped(count, width)],
        (place, factors, texts, other, *images),
        flops=4 * flops,
        scalars=2,
    )
    line = [texts, around(texts, -1), around(texts, 1)]
    line.append(around(line[1], -1))
    passed = other_core(theirs)
    passed, line[1], line[2] = lax.optimization_barrier((passed, line[1], line[2]))
    term = call(add_kernel, [shaped(PLANE, STEPS * per, width)], (mine, passed), scalars=0)
    terms = lax.all_to_all(term, ("x", "z"), 0, 0, tiled=True)
    text_grad = call(sum_kernel, [shaped(STEPS, per, width, dtype=f32)], (factors, terms))

    across = [other] + [other_core(a) for a in line[1:]]
    offsets = [(0, 0), (1, 0), (-1, 0), (2, 0), (0, 1), (-1, 1), (1, 1), (2, 1)]
    image_grad, row_loss = call(
        functools.partial(image_kernel, offsets),
        [shaped(rows, width, dtype=f32), shaped(rows, dtype=f32)],
        (place, factors, image, *line, *across),
        flops=NY * flops,
        scalars=2,
        scratch_shapes=[pltpu.VMEM((len(offsets) * count, width), bf16)],
    )
    return image_grad, text_grad, row_loss


def solution(mesh):
    mesh = Mesh(mesh.devices.reshape(NX, NZ, NY, NC), AXES)
    in_specs = (P(AXES, None), P(AXES, None), P(), P())
    out_specs = (P(AXES, None), P(None, AXES, None), P(AXES))
    return jax.shard_map(local, mesh=mesh, in_specs=in_specs, out_specs=out_specs, check_vma=False)
```
